256 devices in a mesh: depth: 32 (over x_hi, z, core), freq: 8 (over x_lo, y).
Axes of the slice: x: 4 (x_hi: 2, x_lo: 2; x = x_hi * 2 + x_lo), y: 4, z: 8, core: 2. Of those that a mesh axis runs over, the one named last changes fastest.
Arguments:
- propagator: bfloat16 [32, 16, 2, 1024, 1024], P('depth', 'freq'), may hold values from -0.125 to 0.125
- incident: bfloat16 [32, 16, 1024, 256], P('depth', 'freq'), may hold values from -6 to 6
- coeffs: float32 [32, 1024, 64], P('depth'), may hold values from -4 to 4
Outputs:
- upgoing: bfloat16 [32, 16, 1024, 256], P('depth', 'freq')
- gradient: float32 [32, 1024, 64], P('depth', 'freq')
- reflected: bfloat16 [32, 16, 1024, 256], P('depth', 'freq')
The draws below stay inside these ranges and needn't reach their ends.
All inputs are finite; a program needn't handle non-finite values.
Results may differ from the reference program's by a relative error of at most 0.024.
Values may be sent and summed in bfloat16 or wider, within the bound.
No kernel may reach another device: no remote copies, remote signals or barrier semaphores. Data moves between devices by JAX's collectives and lax.ppermute only.
A program may use at most 64 MiB of HBM per device.

```python
import jax
import jax.numpy as jnp
from jax import lax

NX = 1024
NA = 64
SHOTS = 128
ITERS = 3
LEVELS = 32
FREQS = 16


def block_scale(key, extent, cuts, low, top_value):
    def one(position, parts):
        draws = jax.random.uniform(jax.random.fold_in(jax.random.fold_in(key, 6), position), (parts,), jnp.float32, low / len(cuts), top_value / len(cuts))
        return jnp.repeat(jnp.exp(draws), extent[position] // parts).reshape((-1,) + (1,) * (len(extent) - position - 1))

    gain = one(*cuts[0])
    for cut in cuts[1:]:
        gain = gain * one(*cut)
    return gain


def scatter_about(rng, extent, width, limit, pieces=(), kind=jnp.bfloat16):
    drawn = width * jax.random.normal(rng, extent, jnp.float32)
    if pieces:
        drawn = drawn * block_scale(rng, extent, pieces, -0.22, 0.18)
    return jnp.clip(drawn, -limit, limit).astype(kind)


def setup_inputs(seed: int = 0) -> dict:
    streams_of = jax.random.split(jax.random.key(seed), 4)
    propagator = scatter_about(streams_of[0], (LEVELS, FREQS, 2, NX, NX), (2 * NX) ** -0.5, 0.125, ((0, 32), (1, 8)))
    incident = scatter_about(streams_of[1], (LEVELS, FREQS, NX, 2 * SHOTS), 1.0, 6.0, ((0, 32), (1, 8)))
    coeffs = scatter_about(streams_of[2], (LEVELS, NX, NA), 1.0, 4.0, ((0, 32),), jnp.float32)
    return {"propagator": propagator, "incident": incident, "coeffs": coeffs}


def angle_table():
    angle = jnp.arange(NA, dtype=jnp.float32)[:, None] + 0.5
    place = jnp.arange(NX, dtype=jnp.float32)[None, :] + 0.5
    return (jnp.sqrt(2.0 / NX) * jnp.cos(jnp.pi * angle * place / NX)).astype(jnp.bfloat16)

def angles_of(table, field):
    return jnp.einsum('ay,lfys->lfas', table.astype(jnp.float32), field.astype(jnp.float32)).astype(jnp.bfloat16)

def reflect(kernel, table, field):
    return jnp.einsum('lxa,lfas->lfxs', kernel.astype(jnp.float32), angles_of(table, field).astype(jnp.float32))

def apply_level(weights, field, transpose):
    wf = weights.astype(jnp.float32)
    ff = field.astype(jnp.float32)
    form = 'fyx,fys->fxs' if transpose else 'fxy,fys->fxs'
    first = jnp.einsum(form, wf[:, 0], ff)
    second = jnp.einsum(form, wf[:, 1], ff)
    return first + jnp.concatenate([-second[..., SHOTS:], second[..., :SHOTS]], -1)

def propagate(propagator, field, transpose):
    return lax.map(lambda pair: apply_level(pair[0], pair[1], transpose), (propagator, field))

def reference(propagator, incident, coeffs):
    table = angle_table()
    kernel = (coeffs * table.T.astype(jnp.float32)[None]).astype(jnp.bfloat16)
    down = jnp.zeros(incident.shape, jnp.bfloat16)
    upgoing = jnp.zeros(incident.shape, jnp.bfloat16)
    for step in range(ITERS):
        send_down = (down.astype(jnp.float32) - reflect(kernel, table, upgoing)).astype(jnp.bfloat16)
        total = (incident.astype(jnp.float32) + down.astype(jnp.float32)).astype(jnp.bfloat16)
        send_up = (upgoing.astype(jnp.float32) + reflect(kernel, table, total)).astype(jnp.bfloat16)
        blank = jnp.zeros_like(send_down[:1])
        above = jnp.concatenate([blank, send_down[:-1]], 0)
        below = jnp.concatenate([send_up[1:], blank], 0)
        down = propagate(propagator, above, False).astype(jnp.bfloat16)
        upgoing = propagate(propagator, below, True).astype(jnp.bfloat16)
    total = (incident.astype(jnp.float32) + down.astype(jnp.float32)).astype(jnp.bfloat16)
    final_angles = angles_of(table, total)
    summed = jnp.einsum('lfxs,lfas->lxa', upgoing.astype(jnp.float32), final_angles.astype(jnp.float32))
    gradient = summed / jnp.sqrt(jnp.float32(SHOTS * FREQS))
    updated = coeffs - gradient
    new_kernel = (updated * table.T.astype(jnp.float32)[None]).astype(jnp.bfloat16)
    reflected = jnp.einsum('lxa,lfas->lfxs', new_kernel.astype(jnp.float32), final_angles.astype(jnp.float32)).astype(jnp.bfloat16)
    return (upgoing, gradient, reflected)
```

```python
import jax
import jax.numpy as jnp
from jax import lax
from jax.sharding import PartitionSpec as P

BF = jnp.bfloat16
F32 = jnp.float32


def passed_along(block, axis, distance):
    devices = range(lax.axis_size(axis))
    route = [(i - distance, i) for i in devices if i - distance in devices]
    return lax.ppermute(block, axis, route)


def angle_table(count, points):
    angle = jnp.arange(count, dtype=F32)[:, None] + 0.5
    place = jnp.arange(points, dtype=F32)[None, :] + 0.5
    return (jnp.sqrt(2.0 / points) * jnp.cos(jnp.pi * angle * place / points)).astype(BF)


def dot(form, a, b):
    return jnp.einsum(form, a, b, preferred_element_type=F32)


def turned(field):
    half = field.shape[-1] // 2
    return jnp.concatenate([-field[..., half:], field[..., :half]], -1)


def both(field):
    return jnp.concatenate([field, turned(field)], -2)


def times(pair, field):
    return dot("fab,fbs->fas", pair, both(field))


def joined(panel):
    nfreq, _, count, points = panel.shape
    return panel.reshape(nfreq, 2 * count, points)


def advance(weights, panel):
    real, imag = panel[:, 0], panel[:, 1]
    left = jnp.concatenate(
        [jnp.concatenate([real, -imag], -1), jnp.concatenate([imag, real], -1)], 1
    )
    nfreq, _, rows, points = weights.shape
    out = dot("fax,fxy->fay", left, weights.reshape(nfreq, 2 * rows, points)).astype(BF)
    return out.reshape(nfreq, 2, -1, points)


def summed(value, axis):
    size = lax.axis_size(axis)
    step = size // 2
    while step:
        small = value.astype(BF)
        other = lax.ppermute(small, axis, [(i, i ^ step) for i in range(size)])
        value = small.astype(F32) + other.astype(F32)
        step //= 2
    return value


def local(propagator, incident, coeffs):
    weights = propagator[0]
    source = incident[0]
    count = coeffs.shape[2]
    points = incident.shape[2]
    width = incident.shape[3]
    nfreq = source.shape[0]
    table = angle_table(count, points)
    kernel = (coeffs[0].T * table.astype(F32)).astype(BF)

    def up(x):
        return passed_along(x, "depth", -1)

    def down(x):
        return passed_along(x, "depth", 1)

    start = dot("ax,fxs->fas", table, source).astype(BF)
    kernel_below = up(kernel)
    start1 = up(start)
    kernel_above = down(kernel)
    seen = dot("ax,fcxy->fcay", table, weights).astype(BF)
    m = dot("ax,fcxy->fcay", kernel_below, weights).astype(BF)
    m_below = up(m)
    start2 = up(start1)
    j = dot("fcxy,ay->fxca", weights, kernel_above).astype(BF).reshape(nfreq, points, 2 * count)
    j_above = down(j)
    g = dot("fcax,bx->facb", seen, kernel_above).astype(BF).reshape(nfreq, count, 2 * count)
    g_below = up(g)
    tm = dot("ax,fbx->fab", table, joined(m)).astype(BF)
    tu1 = times(tm, start1).astype(BF)
    tu1_above = down(tu1)
    n = advance(weights, m_below)
    n_below = up(n)
    start3 = up(start2)
    tn = dot("ax,fbx->fab", table, joined(n)).astype(BF)
    tu2 = (times(tn, start2) + times(tm, start1)).astype(BF)
    tu2_above = down(tu2)
    tu1_above2 = down(tu1_above)
    part_r = dot("fax,fxb->fab", seen[:, 0], j_above)
    part_i = dot("fax,fxb->fab", seen[:, 1], j_above)
    h = (part_r + turned(part_i)).astype(BF)
    td3 = times(h, tu1_above2) + times(g, tu2_above)
    final_angles = (start.astype(F32) - td3).astype(BF)
    b1 = (start1.astype(F32) - times(g_below, tu1)).astype(BF)
    q = advance(weights, n_below)
    panels = jnp.concatenate([joined(q), joined(n), joined(m)], 1)
    fields = jnp.concatenate([both(start3), both(start2), both(b1)], 1)
    upgoing = dot("fbx,fbs->fxs", panels, fields).astype(BF)

    scale = 1.0 / jnp.sqrt(jnp.float32(width // 2 * nfreq * lax.axis_size("freq")))
    gradient = summed(dot("fas,fxs->ax", final_angles, upgoing) * scale, "freq")
    rows = points // lax.axis_size("freq")
    grad_rows = lax.dynamic_slice_in_dim(gradient, lax.axis_index("freq") * rows, rows, 1).T
    new_kernel = ((coeffs[0].T - gradient) * table.astype(F32)).astype(BF)
    reflected = dot("ax,fas->fxs", new_kernel, final_angles).astype(BF)
    return (upgoing[None], grad_rows[None], reflected[None])


def solution(mesh):
    return jax.shard_map(
        local,
        mesh=mesh,
        in_specs=(
            P("depth", "freq", None, None, None),
            P("depth", "freq", None, None),
            P("depth", None, None),
        ),
        out_specs=(
            P("depth", "freq", None, None),
            P("depth", "freq", None),
            P("depth", "freq", None, None),
        ),
        check_vma=False,
    )
```

```python
import jax
import jax.numpy as jnp
import numpy as np
from jax import lax
from jax.experimental import pallas as pl
from jax.experimental.pallas import tpu as pltpu
from jax.sharding import PartitionSpec as P

BF = jnp.bfloat16
F32 = jnp.float32
MIB = 2**20


def exchanged(block, axis, first):
    size = lax.axis_size(axis)
    route = []
    for i in range(first, size - 1, 2):
        route += [(i, i + 1), (i + 1, i)]
    return lax.ppermute(block, axis, route)


def is_even(axis):
    return lax.rem(lax.axis_index(axis), 2) == 0


def angle_table(count, points):
    angle = np.arange(count, dtype=np.float32)[:, None] + np.float32(0.5)
    place = np.arange(points, dtype=np.float32)[None, :] + np.float32(0.5)
    wave = np.cos(np.float32(np.pi) * angle * place / np.float32(points))
    return jnp.asarray((np.sqrt(np.float32(2.0 / points)) * wave).astype(BF))


def dot(a, b):
    return jnp.dot(a, b, preferred_element_type=F32)


def dot_t(a, b):
    return lax.dot_general(a, b, (((1,), (1,)), ((), ())), preferred_element_type=F32)


def t_dot(a, b):
    return lax.dot_general(a, b, (((0,), (0,)), ((), ())), preferred_element_type=F32)


def turned(field):
    half = field.shape[-1] // 2
    return jnp.concatenate([-field[:, half:], field[:, :half]], -1)


def both(field):
    return jnp.concatenate([field, turned(field)], 0)


def pack(ref, row, col, value):
    width = value.shape[1]
    fold = min((ref.shape[1] - col) // width, value.shape[0] // 16)
    rows = value.shape[0] // fold
    for i in range(fold):
        ref[row : row + rows, col + i * width : col + (i + 1) * width] = value[
            i * rows : (i + 1) * rows
        ]


def unpack(ref, row, col, count, width):
    fold = min((ref.shape[1] - col) // width, count // 16)
    rows = count // fold
    return jnp.concatenate(
        [
            ref[row : row + rows, col + i * width : col + (i + 1) * width]
            for i in range(fold)
        ],
        0,
    )


def folded_rows(count, width, points):
    return count // min(points // width, count // 16)


def call(body, outs, args, flops, vmem=12, scratch=(), hbm=()):
    spec = pl.BlockSpec(memory_space=pltpu.VMEM)
    anywhere = pl.BlockSpec(memory_space=pltpu.HBM)
    size = sum(int(np.prod(a.shape)) * a.dtype.itemsize for a in args)
    return pl.pallas_call(
        body,
        out_shape=outs,
        in_specs=[anywhere if i in hbm else spec for i in range(len(args))],
        out_specs=[spec] * len(outs),
        scratch_shapes=list(scratch),
        cost_estimate=pl.CostEstimate(flops=flops, bytes_accessed=size, transcendentals=0),
        compiler_params=pltpu.CompilerParams(vmem_limit_bytes=vmem * MIB),
    )(*args)


def shape(*dims, dtype=BF):
    return jax.ShapeDtypeStruct(dims, dtype)


def local(propagator, incident, coeffs):
    weights = propagator[0]
    source = incident[0]
    coeffs = coeffs[0].T
    count, points = coeffs.shape
    nfreq, _, width = source.shape
    table = angle_table(count, points)
    panel = 2 * count
    rows = folded_rows(count, width, points)
    total = nfreq * rows
    spread = panel * (count // 16)
    near = points * count * panel * nfreq * 2
    whole = nfreq * 2 * points * points * panel * 2

    def swap(x, y):
        far = exchanged(y, "depth", 1)
        near = exchanged(x, "depth", 0)
        return near, far

    def from_below(near_ref, far_ref, low, high):
        return jnp.where(is_even("depth"), near_ref[low:high], far_ref[low:high])

    def from_above(near_ref, far_ref, low, high):
        return jnp.where(is_even("depth"), far_ref[low:high], near_ref[low:high])

    hbm = pltpu.HBM

    def first(s_ref, c_ref, t_ref, out, table_out, src, coef, sems):
        copies = [
            pltpu.make_async_copy(t_ref, table_out, sems.at[0]),
            pltpu.make_async_copy(c_ref, coef, sems.at[1]),
            pltpu.make_async_copy(s_ref, src, sems.at[2]),
        ]
        for copy in copies:
            copy.start()
        copies[0].wait()
        copies[1].wait()
        out[0:count] = (coef[...] * table_out[...].astype(F32)).astype(BF)
        copies[2].wait()
        for f in range(nfreq):
            pack(out, count + f * rows, 0, dot(table_out[...], src[f]).astype(BF))

    own1, table = call(
        first,
        [shape(count + total, points), pltpu.VMEM((count, points), BF)],
        [pltpu.with_memory_space_constraint(x, hbm) for x in (source, coeffs, table)],
        near,
        scratch=[
            pltpu.VMEM(source.shape, BF),
            pltpu.VMEM(coeffs.shape, F32),
            pltpu.SemaphoreType.DMA((3,)),
        ],
        hbm=(0, 1, 2),
    )
    near1, far1 = swap(own1, own1)

    def load(w_ref, t_ref, kept, seen, sems):
        copies = [
            pltpu.make_async_copy(w_ref.at[f, c], kept.at[f, c], sems.at[2 * f + c])
            for f in range(nfreq)
            for c in range(2)
        ]
        for copy in copies:
            copy.start()
        for f in range(nfreq):
            for c in range(2):
                copies[2 * f + c].wait()
                seen[f, c * count : (c + 1) * count] = dot(t_ref[...], kept[f, c]).astype(BF)

    kept, seen = call(
        load,
        [pltpu.VMEM(weights.shape, BF), shape(nfreq, panel, points)],
        [pltpu.with_memory_space_constraint(weights, hbm), table],
        whole // 2,
        scratch=[pltpu.SemaphoreType.DMA((2 * nfreq,))],
        hbm=(0,),
    )
    body = nfreq * panel

    def make_m(w_ref, t_ref, near_ref, far_ref, out, tm):
        kernel = from_below(near_ref, far_ref, 0, count)
        for f in range(nfreq):
            for c in range(2):
                row = f * panel + c * count
                out[row : row + count] = dot(kernel, w_ref[f, c]).astype(BF)
        out[body : body + total] = from_below(near_ref, far_ref, count, count + total)
        for f in range(nfreq):
            pair = dot_t(t_ref[...], out[f * panel : (f + 1) * panel]).astype(BF)
            tm[f] = pair
            start1 = unpack(out, body + f * rows, 0, count, width)
            pack(out, body + total + f * rows, 0, dot(pair, both(start1)).astype(BF))

    own2, tm = call(
        make_m,
        [shape(body + 2 * total, points), shape(nfreq, count, panel)],
        [kept, table, near1, far1],
        whole // 2,
    )
    near2, far2 = swap(own2, own2)

    def make_j(w_ref, near_ref, far_ref, s_ref, own_ref, out, g_out):
        kernel = from_above(near_ref, far_ref, 0, count)
        zero = jnp.zeros((count, points), BF)
        left = jnp.concatenate([kernel, zero], 0)
        right = jnp.concatenate([zero, kernel], 0)
        for f in range(nfreq):
            for c in range(2):
                row = f * panel + c * count
                out[row : row + count] = dot_t(kernel, w_ref[f, c]).astype(BF)
            g_out[f] = (
                dot_t(s_ref[f, 0:count], left) + dot_t(s_ref[f, count:panel], right)
            ).astype(BF)

    j, g = call(
        make_j,
        [shape(body, points), shape(nfreq, count, panel)],
        [kept, near1, far1, seen, own2],
        whole // 2,
    )

    def advance(w_ref, x, f):
        y = jnp.concatenate([-x[count:], x[:count]], 0)
        return (dot(x, w_ref[f, 0]) + dot(y, w_ref[f, 1])).astype(BF)

    def make_n(w_ref, t_ref, near_ref, far_ref, own_ref, tm_ref, j_ref, g_ref, out, x_out, y_out):
        for f in range(nfreq):
            m = from_below(near_ref, far_ref, f * panel, (f + 1) * panel)
            out[f * panel : (f + 1) * panel] = advance(w_ref, m, f)
        out[body : body + total] = from_below(near_ref, far_ref, body, body + total)

        def fill(up, down):
            up[0 : body + total] = out[...]
            down[0:body] = j_ref[...]
            down[body : body + total] = from_above(
                near_ref, far_ref, body + total, body + 2 * total
            )
            for f in range(nfreq):
                pack(up, body + total, f * spread, g_ref[f])
                pair = dot_t(t_ref[...], out[f * panel : (f + 1) * panel]).astype(BF)
                start1 = unpack(own_ref, body + f * rows, 0, count, width)
                start2 = unpack(out, body + f * rows, 0, count, width)
                value = dot(pair, both(start2)) + dot(tm_ref[f], both(start1))
                pack(down, body + total + f * rows, 0, value.astype(BF))

        @pl.when(is_even("depth"))
        def _():
            fill(y_out, x_out)

        @pl.when(jnp.logical_not(is_even("depth")))
        def _():
            fill(x_out, y_out)

    own3, x3, y3 = call(
        make_n,
        [
            shape(body + total, points),
            shape(body + 2 * total, points),
            shape(body + 2 * total, points),
        ],
        [kept, table, near2, far2, own2, tm, j, g],
        whole,
    )
    near3, far3 = swap(x3, y3)

    scale = float(1.0 / np.sqrt(np.float32(width // 2 * nfreq * lax.axis_size("freq"))))

    def make_q(
        w_ref, near_ref, far_ref, n_ref, m_ref, s_ref, g_ref, o_ref, q_out, f_out, c_out, a_out
    ):
        partial = jnp.zeros((count, points), F32)
        tail = from_below(near_ref, far_ref, body, body + 2 * total)
        above = from_above(near_ref, far_ref, body, body + 2 * total)
        for f in range(nfreq):
            j = from_above(near_ref, far_ref, f * panel, (f + 1) * panel)
            real = dot_t(s_ref[f, 0:count], j)
            imag = dot_t(s_ref[f, count:panel], j)
            h = (real + turned(imag)).astype(BF)
            tu1_two = unpack(above, f * rows, 0, count, width)
            tu2_one = unpack(above, total + f * rows, 0, count, width)
            down3 = dot(h, both(tu1_two)) + dot(g_ref[f], both(tu2_one))
            start = unpack(o_ref, count + f * rows, 0, count, width)
            angles = (start.astype(F32) - down3).astype(BF)
            a_out[f] = angles

            n = from_below(near_ref, far_ref, f * panel, (f + 1) * panel)
            q = advance(w_ref, n, f)
            q_out[f] = q
            low = body + f * rows
            start1 = unpack(m_ref, low, 0, count, width)
            start2 = unpack(n_ref, low, 0, count, width)
            start3 = unpack(tail, f * rows, 0, count, width)
            turn = unpack(tail, total, f * spread, count, panel)
            down2 = dot(turn, both(unpack(m_ref, low + total, 0, count, width)))
            shifted = (start1.astype(F32) - down2).astype(BF)
            fields = jnp.concatenate([both(start3), both(start2), both(shifted)], 0)
            f_out[f] = fields
            weight = dot_t(angles, fields).astype(BF)
            stack = jnp.concatenate(
                [q, n_ref[f * panel : (f + 1) * panel], m_ref[f * panel : (f + 1) * panel]], 0
            )
            partial = partial + dot(weight, stack)
        c_out[...] = (partial * scale).astype(BF)

    q, fields, partial, angles = call(
        make_q,
        [
            shape(nfreq, panel, points),
            shape(nfreq, 3 * panel, width),
            shape(count, points),
            shape(nfreq, count, width),
        ],
        [kept, near3, far3, own3, own2, seen, g, own1],
        whole + 5 * near,
    )

    def make_up(q_ref, n_ref, m_ref, f_ref, out):
        for f in range(nfreq):
            stack = jnp.concatenate(
                [
                    q_ref[f],
                    n_ref[f * panel : (f + 1) * panel],
                    m_ref[f * panel : (f + 1) * panel],
                ],
                0,
            )
            out[f] = t_dot(stack, f_ref[f]).astype(BF)

    (upgoing,) = call(
        make_up, [shape(nfreq, points, width)], [q, own3, own2, fields], 3 * near
    )

    size = lax.axis_size("freq")
    share = points // size
    value = partial
    steps = [step for step in (4, 1, 3) if step < size]
    for step in steps:
        other = lax.ppermute(value, "freq", [(i, i ^ step) for i in range(size)])
        if step != steps[-1]:
            value = (value.astype(F32) + other.astype(F32)).astype(BF)

    def last(c_ref, t_ref, v_ref, o_ref, a_ref, out, g_out, keep):
        gradient = v_ref[...].astype(F32) + o_ref[...].astype(F32)
        keep[...] = gradient
        kernel = ((c_ref[...] - gradient) * t_ref[...].astype(F32)).astype(BF)
        for f in range(nfreq):
            out[f] = t_dot(kernel, a_ref[f]).astype(BF)
        begin = pl.multiple_of(lax.axis_index("freq") * share, share)
        g_out[...] = keep[:, pl.ds(begin, share)]

    reflected, mine = call(
        last,
        [shape(nfreq, points, width), shape(count, share, dtype=F32)],
        [coeffs, table, value, other, angles],
        near,
        scratch=[pltpu.VMEM((count, points), F32)],
    )
    return (upgoing[None], mine.T[None], reflected[None])


def solution(mesh):
    return jax.shard_map(
        local,
        mesh=mesh,
        in_specs=(
            P("depth", "freq", None, None, None),
            P("depth", "freq", None, None),
            P("depth", None, None),
        ),
        out_specs=(
            P("depth", "freq", None, None),
            P("depth", "freq", None),
            P("depth", "freq", None, None),
        ),
        check_vma=False,
    )
```

```python
import jax
import jax.numpy as jnp
import numpy as np
from jax import lax
from jax.experimental import pallas as pl
from jax.experimental.pallas import tpu as pltpu
from jax.sharding import PartitionSpec as P

BF = jnp.bfloat16
F32 = jnp.float32
MIB = 2**20


def exchanged(block, axis, first):
    size = lax.axis_size(axis)
    route = []
    for i in range(first, size - 1, 2):
        route += [(i, i + 1), (i + 1, i)]
    return lax.ppermute(block, axis, route)


def is_even(axis):
    return lax.rem(lax.axis_index(axis), 2) == 0


def angle_table(count, points):
    angle = np.arange(count, dtype=np.float32)[:, None] + np.float32(0.5)
    place = np.arange(points, dtype=np.float32)[None, :] + np.float32(0.5)
    wave = np.cos(np.float32(np.pi) * angle * place / np.float32(points))
    return jnp.asarray((np.sqrt(np.float32(2.0 / points)) * wave).astype(BF))


def dot(a, b):
    return jnp.dot(a, b, preferred_element_type=F32)


def dot_t(a, b):
    return lax.dot_general(a, b, (((1,), (1,)), ((), ())), preferred_element_type=F32)


def t_dot(a, b):
    return lax.dot_general(a, b, (((0,), (0,)), ((), ())), preferred_element_type=F32)


def turned(field):
    half = field.shape[-1] // 2
    return jnp.concatenate([-field[:, half:], field[:, :half]], -1)


def both(field):
    return jnp.concatenate([field, turned(field)], 0)


def pack(ref, row, col, value):
    width = value.shape[1]
    fold = min((ref.shape[1] - col) // width, value.shape[0] // 16)
    rows = value.shape[0] // fold
    for i in range(fold):
        ref[row : row + rows, col + i * width : col + (i + 1) * width] = value[
            i * rows : (i + 1) * rows
        ]


def unpack(ref, row, col, count, width):
    fold = min((ref.shape[1] - col) // width, count // 16)
    rows = count // fold
    return jnp.concatenate(
        [
            ref[row : row + rows, col + i * width : col + (i + 1) * width]
            for i in range(fold)
        ],
        0,
    )


def folded_rows(count, width, points):
    return count // min(points // width, count // 16)


def call(body, outs, args, flops, vmem=12, scratch=(), hbm=()):
    spec = pl.BlockSpec(memory_space=pltpu.VMEM)
    anywhere = pl.BlockSpec(memory_space=pltpu.HBM)
    size = sum(int(np.prod(a.shape)) * a.dtype.itemsize for a in args)
    return pl.pallas_call(
        body,
        out_shape=outs,
        in_specs=[anywhere if i in hbm else spec for i in range(len(args))],
        out_specs=[spec] * len(outs),
        scratch_shapes=list(scratch),
        cost_estimate=pl.CostEstimate(flops=flops, bytes_accessed=size, transcendentals=0),
        compiler_params=pltpu.CompilerParams(vmem_limit_bytes=vmem * MIB),
    )(*args)


def shape(*dims, dtype=BF):
    return jax.ShapeDtypeStruct(dims, dtype)


def local(propagator, incident, coeffs):
    weights = propagator[0]
    source = incident[0]
    coeffs = coeffs[0].T
    count, points = coeffs.shape
    nfreq, _, width = source.shape
    table = angle_table(count, points)
    panel = 2 * count
    rows = folded_rows(count, width, points)
    total = nfreq * rows
    spread = panel * (count // 16)
    near = points * count * panel * nfreq * 2
    whole = nfreq * 2 * points * points * panel * 2

    def swap(x, y):
        far = exchanged(y, "depth", 1)
        near = exchanged(x, "depth", 0)
        return near, far

    def from_below(near_ref, far_ref, low, high):
        return jnp.where(is_even("depth"), near_ref[low:high], far_ref[low:high])

    def from_above(near_ref, far_ref, low, high):
        return jnp.where(is_even("depth"), far_ref[low:high], near_ref[low:high])

    hbm = pltpu.HBM

    def first(s_ref, c_ref, t_ref, out, table_out, src, coef, sems):
        copies = [
            pltpu.make_async_copy(t_ref, table_out, sems.at[0]),
            pltpu.make_async_copy(c_ref, coef, sems.at[1]),
            pltpu.make_async_copy(s_ref, src, sems.at[2]),
        ]
        for copy in copies:
            copy.start()
        copies[0].wait()
        copies[1].wait()
        out[0:count] = (coef[...] * table_out[...].astype(F32)).astype(BF)
        copies[2].wait()
        for f in range(nfreq):
            pack(out, count + f * rows, 0, dot(table_out[...], src[f]).astype(BF))

    own1, table = call(
        first,
        [shape(count + total, points), pltpu.VMEM((count, points), BF)],
        [pltpu.with_memory_space_constraint(x, hbm) for x in (source, coeffs, table)],
        near,
        scratch=[
            pltpu.VMEM(source.shape, BF),
            pltpu.VMEM(coeffs.shape, F32),
            pltpu.SemaphoreType.DMA((3,)),
        ],
        hbm=(0, 1, 2),
    )
    near1, far1 = swap(own1, own1)

    def load(w_ref, t_ref, kept, seen, sems):
        copies = [
            pltpu.make_async_copy(w_ref.at[f, c], kept.at[f, c], sems.at[2 * f + c])
            for f in range(nfreq)
            for c in range(2)
        ]
        for copy in copies:
            copy.start()
        for f in range(nfreq):
            for c in range(2):
                copies[2 * f + c].wait()
                seen[f, c * count : (c + 1) * count] = dot(t_ref[...], kept[f, c]).astype(BF)

    kept, seen = call(
        load,
        [pltpu.VMEM(weights.shape, BF), shape(nfreq, panel, points)],
        [pltpu.with_memory_space_constraint(weights, hbm), table],
        whole // 2,
        scratch=[pltpu.SemaphoreType.DMA((2 * nfreq,))],
        hbm=(0,),
    )
    body = nfreq * panel

    height = body + total + 16

    def make_m(w_ref, t_ref, near_ref, far_ref, out, tm):
        kernel = from_below(near_ref, far_ref, 0, count)
        out[body : body + total] = from_below(near_ref, far_ref, count, count + total)
        for f in range(nfreq):
            parts = [dot(kernel, w_ref[f, c]).astype(BF) for c in range(2)]
            m = jnp.concatenate(parts, 0)
            out[f * panel : (f + 1) * panel] = m
            pair = dot_t(t_ref[...], m).astype(BF)
            tm[f] = pair
            pack(out, body + total, f * spread, pair)

    own2, tm = call(
        make_m,
        [shape(height, points), shape(nfreq, count, panel)],
        [kept, table, near1, far1],
        whole // 2,
    )
    near2, far2 = swap(own2, own2)

    def make_j(w_ref, near_ref, far_ref, s_ref, own_ref, tm_ref, out, g_out, u_out):
        kernel = from_above(near_ref, far_ref, 0, count)
        zero = jnp.zeros((count, points), BF)
        left = jnp.concatenate([kernel, zero], 0)
        right = jnp.concatenate([zero, kernel], 0)
        for f in range(nfreq):
            for c in range(2):
                row = f * panel + c * count
                out[row : row + count] = dot_t(kernel, w_ref[f, c]).astype(BF)
            g_out[f] = (
                dot_t(s_ref[f, 0:count], left) + dot_t(s_ref[f, count:panel], right)
            ).astype(BF)
            start1 = unpack(own_ref, body + f * rows, 0, count, width)
            u_out[f] = dot(tm_ref[f], both(start1)).astype(BF)

    j, g, tu1 = call(
        make_j,
        [
            shape(body, points),
            shape(nfreq, count, panel),
            shape(nfreq, count, width),
        ],
        [kept, near1, far1, seen, own2, tm],
        whole // 2,
    )

    def advance(w_ref, x, f):
        y = jnp.concatenate([-x[count:], x[:count]], 0)
        return (dot(x, w_ref[f, 0]) + dot(y, w_ref[f, 1])).astype(BF)

    def make_n(w_ref, t_ref, near_ref, far_ref, o_ref, j_ref, g_ref, out, x_out, y_out, u_out):
        even = is_even("depth")
        low = body + total

        def put(row, col, up, down):
            place = (slice(row, row + up.shape[0]), slice(col, col + up.shape[1]))
            x_out[place] = jnp.where(even, down, up)
            y_out[place] = jnp.where(even, up, down)

        angles = from_below(near_ref, far_ref, body, low)
        out[body:] = angles
        above = from_above(near_ref, far_ref, low, height)
        for f in range(nfreq):
            first_row = f * panel
            x = from_below(near_ref, far_ref, first_row, first_row + panel)
            n = advance(w_ref, x, f)
            out[first_row : first_row + panel] = n
            put(first_row, 0, n, j_ref[first_row : first_row + panel])
            pair = dot_t(t_ref[...], n).astype(BF)
            for i in range(count // 16):
                cut = slice(i * 16, (i + 1) * 16)
                put(low, f * spread + i * panel, g_ref[f, cut], pair[cut])
            start = unpack(o_ref, count + f * rows, 0, count, width)
            pair_above = unpack(above, 0, f * spread, count, panel)
            seen_above = dot(pair_above, both(start)).astype(BF)
            u_out[f] = seen_above
            for i in range(count // rows):
                cut = slice(i * rows, (i + 1) * rows)
                up = angles[f * rows : (f + 1) * rows, i * width : (i + 1) * width]
                put(body + f * rows, i * width, up, seen_above[cut])

    own3, x3, y3, tu1_above = call(
        make_n,
        [
            shape(body + total, points),
            shape(height, points),
            shape(height, points),
            shape(nfreq, count, width),
        ],
        [kept, table, near2, far2, own1, j, g],
        whole,
    )
    near3, far3 = swap(x3, y3)

    scale = float(1.0 / np.sqrt(np.float32(width // 2 * nfreq * lax.axis_size("freq"))))

    def make_q(
        w_ref, near_ref, far_ref, n_ref, m_ref, s_ref, g_ref, o_ref, u_ref, v_ref,
        q_out, f_out, c_out, a_out
    ):
        partial = jnp.zeros((count, points), F32)
        tail = from_below(near_ref, far_ref, body, height)
        above = from_above(near_ref, far_ref, body, height)
        for f in range(nfreq):
            j = from_above(near_ref, far_ref, f * panel, (f + 1) * panel)
            real = dot_t(s_ref[f, 0:count], j)
            imag = dot_t(s_ref[f, count:panel], j)
            h = (real + turned(imag)).astype(BF)
            tu1_two = unpack(above, f * rows, 0, count, width)
            low = body + f * rows
            start1 = unpack(m_ref, low, 0, count, width)
            pair = unpack(above, total, f * spread, count, panel)
            tu2_one = (dot(pair, both(start1)) + v_ref[f].astype(F32)).astype(BF)
            down3 = dot(h, both(tu1_two)) + dot(g_ref[f], both(tu2_one))
            start = unpack(o_ref, count + f * rows, 0, count, width)
            angles = (start.astype(F32) - down3).astype(BF)
            a_out[f] = angles

            n = from_below(near_ref, far_ref, f * panel, (f + 1) * panel)
            q = advance(w_ref, n, f)
            q_out[f] = q
            start2 = unpack(n_ref, low, 0, count, width)
            start3 = unpack(tail, f * rows, 0, count, width)
            turn = unpack(tail, total, f * spread, count, panel)
            down2 = dot(turn, both(u_ref[f]))
            shifted = (start1.astype(F32) - down2).astype(BF)
            fields = jnp.concatenate([both(start3), both(start2), both(shifted)], 0)
            f_out[f] = fields
            weight = dot_t(angles, fields).astype(BF)
            stack = jnp.concatenate(
                [q, n_ref[f * panel : (f + 1) * panel], m_ref[f * panel : (f + 1) * panel]], 0
            )
            partial = partial + dot(weight, stack)
        c_out[...] = (partial * scale).astype(BF)

    q, fields, partial, angles = call(
        make_q,
        [
            shape(nfreq, panel, points),
            shape(nfreq, 3 * panel, width),
            shape(count, points),
            shape(nfreq, count, width),
        ],
        [kept, near3, far3, own3, own2, seen, g, own1, tu1, tu1_above],
        whole + 5 * near,
    )

    def make_up(q_ref, n_ref, m_ref, f_ref, out):
        for f in range(nfreq):
            stack = jnp.concatenate(
                [
                    q_ref[f],
                    n_ref[f * panel : (f + 1) * panel],
                    m_ref[f * panel : (f + 1) * panel],
                ],
                0,
            )
            out[f] = t_dot(stack, f_ref[f]).astype(BF)

    (upgoing,) = call(
        make_up, [shape(nfreq, points, width)], [q, own3, own2, fields], 3 * near
    )

    size = lax.axis_size("freq")
    share = points // size
    value = partial
    steps = [step for step in (4, 1, 3) if step < size]
    for step in steps:
        other = lax.ppermute(value, "freq", [(i, i ^ step) for i in range(size)])
        if step != steps[-1]:
            value = (value.astype(F32) + other.astype(F32)).astype(BF)

    def last(c_ref, t_ref, v_ref, o_ref, a_ref, out, g_out, keep):
        gradient = v_ref[...].astype(F32) + o_ref[...].astype(F32)
        keep[...] = gradient
        kernel = ((c_ref[...] - gradient) * t_ref[...].astype(F32)).astype(BF)
        for f in range(nfreq):
            out[f] = t_dot(kernel, a_ref[f]).astype(BF)
        begin = pl.multiple_of(lax.axis_index("freq") * share, share)
        g_out[...] = keep[:, pl.ds(begin, share)]

    reflected, mine = call(
        last,
        [shape(nfreq, points, width), shape(count, share, dtype=F32)],
        [coeffs, table, value, other, angles],
        near,
        scratch=[pltpu.VMEM((count, points), F32)],
    )
    return (upgoing[None], mine.T[None], reflected[None])


def solution(mesh):
    return jax.shard_map(
        local,
        mesh=mesh,
        in_specs=(
            P("depth", "freq", None, None, None),
            P("depth", "freq", None, None),
            P("depth", None, None),
        ),
        out_specs=(
            P("depth", "freq", None, None),
            P("depth", "freq", None),
            P("depth", "freq", None, None),
        ),
        check_vma=False,
    )
```

```python
import jax
import jax.numpy as jnp
import numpy as np
from jax import lax
from jax.experimental import pallas as pl
from jax.experimental.pallas import tpu as pltpu
from jax.sharding import PartitionSpec as P

BF = jnp.bfloat16
F32 = jnp.float32
MIB = 2**20


def exchanged(block, axis, first):
    size = lax.axis_size(axis)
    route = []
    for i in range(first, size - 1, 2):
        route += [(i, i + 1), (i + 1, i)]
    return lax.ppermute(block, axis, route)


def is_even(axis):
    return lax.rem(lax.axis_index(axis), 2) == 0


def angle_table(count, points):
    angle = np.arange(count, dtype=np.float32)[:, None] + np.float32(0.5)
    place = np.arange(points, dtype=np.float32)[None, :] + np.float32(0.5)
    wave = np.cos(np.float32(np.pi) * angle * place / np.float32(points))
    return jnp.asarray((np.sqrt(np.float32(2.0 / points)) * wave).astype(BF))


def dot(a, b):
    return jnp.dot(a, b, preferred_element_type=F32)


def dot_t(a, b):
    return lax.dot_general(a, b, (((1,), (1,)), ((), ())), preferred_element_type=F32)


def t_dot(a, b):
    return lax.dot_general(a, b, (((0,), (0,)), ((), ())), preferred_element_type=F32)


def turned(field):
    half = field.shape[-1] // 2
    return jnp.concatenate([-field[:, half:], field[:, :half]], -1)


def both(field):
    return jnp.concatenate([field, turned(field)], 0)


def pack(ref, row, col, value):
    width = value.shape[1]
    fold = min((ref.shape[1] - col) // width, value.shape[0] // 16)
    rows = value.shape[0] // fold
    for i in range(fold):
        ref[row : row + rows, col + i * width : col + (i + 1) * width] = value[
            i * rows : (i + 1) * rows
        ]


def unpack(ref, row, col, count, width):
    fold = min((ref.shape[1] - col) // width, count // 16)
    rows = count // fold
    return jnp.concatenate(
        [
            ref[row : row + rows, col + i * width : col + (i + 1) * width]
            for i in range(fold)
        ],
        0,
    )


def folded_rows(count, width, points):
    return count // min(points // width, count // 16)


def call(body, outs, args, flops, vmem=12, scratch=(), hbm=()):
    spec = pl.BlockSpec(memory_space=pltpu.VMEM)
    anywhere = pl.BlockSpec(memory_space=pltpu.HBM)
    size = sum(int(np.prod(a.shape)) * a.dtype.itemsize for a in args)
    return pl.pallas_call(
        body,
        out_shape=outs,
        in_specs=[anywhere if i in hbm else spec for i in range(len(args))],
        out_specs=[spec] * len(outs),
        scratch_shapes=list(scratch),
        cost_estimate=pl.CostEstimate(flops=flops, bytes_accessed=size, transcendentals=0),
        compiler_params=pltpu.CompilerParams(vmem_limit_bytes=vmem * MIB),
    )(*args)


def shape(*dims, dtype=BF):
    return jax.ShapeDtypeStruct(dims, dtype)


def local(propagator, incident, coeffs):
    weights = propagator[0]
    source = incident[0]
    coeffs = coeffs[0].T
    count, points = coeffs.shape
    nfreq, _, width = source.shape
    table = angle_table(count, points)
    panel = 2 * count
    rows = folded_rows(count, width, points)
    total = nfreq * rows
    spread = panel * (count // 16)
    near = points * count * panel * nfreq * 2
    whole = nfreq * 2 * points * points * panel * 2

    def swap(x, y):
        far = exchanged(y, "depth", 1)
        near = exchanged(x, "depth", 0)
        return near, far

    def from_below(near_ref, far_ref, low, high):
        return jnp.where(is_even("depth"), near_ref[low:high], far_ref[low:high])

    def from_above(near_ref, far_ref, low, high):
        return jnp.where(is_even("depth"), far_ref[low:high], near_ref[low:high])

    hbm = pltpu.HBM

    def first(s_ref, c_ref, t_ref, out, table_out, src, coef, sems):
        copies = [
            pltpu.make_async_copy(t_ref, table_out, sems.at[0]),
            pltpu.make_async_copy(c_ref, coef, sems.at[1]),
            pltpu.make_async_copy(s_ref, src, sems.at[2]),
        ]
        for copy in copies:
            copy.start()
        copies[0].wait()
        copies[1].wait()
        out[0:count] = (coef[...] * table_out[...].astype(F32)).astype(BF)
        copies[2].wait()
        for f in range(nfreq):
            pack(out, count + f * rows, 0, dot(table_out[...], src[f]).astype(BF))

    own1, table = call(
        first,
        [shape(count + total, points), pltpu.VMEM((count, points), BF)],
        [pltpu.with_memory_space_constraint(x, hbm) for x in (source, coeffs, table)],
        near,
        scratch=[
            pltpu.VMEM(source.shape, BF),
            pltpu.VMEM(coeffs.shape, F32),
            pltpu.SemaphoreType.DMA((3,)),
        ],
        hbm=(0, 1, 2),
    )
    near1, far1 = swap(own1, own1)

    def load(w_ref, t_ref, kept, seen, sems):
        copies = [
            pltpu.make_async_copy(w_ref.at[f, c], kept.at[f, c], sems.at[2 * f + c])
            for f in range(nfreq)
            for c in range(2)
        ]
        for copy in copies:
            copy.start()
        for f in range(nfreq):
            for c in range(2):
                copies[2 * f + c].wait()
                seen[f, c * count : (c + 1) * count] = dot(t_ref[...], kept[f, c]).astype(BF)

    kept, seen = call(
        load,
        [pltpu.VMEM(weights.shape, BF), shape(nfreq, panel, points)],
        [pltpu.with_memory_space_constraint(weights, hbm), table],
        whole // 2,
        scratch=[pltpu.SemaphoreType.DMA((2 * nfreq,))],
        hbm=(0,),
    )
    body = nfreq * panel

    height = body + total + 16

    def make_m(w_ref, t_ref, near_ref, far_ref, out, tm):
        kernel = from_below(near_ref, far_ref, 0, count)
        out[body : body + total] = from_below(near_ref, far_ref, count, count + total)
        for f in range(nfreq):
            parts = [dot(kernel, w_ref[f, c]).astype(BF) for c in range(2)]
            m = jnp.concatenate(parts, 0)
            out[f * panel : (f + 1) * panel] = m
            pair = dot_t(t_ref[...], m).astype(BF)
            tm[f] = pair
            pack(out, body + total, f * spread, pair)

    own2, tm = call(
        make_m,
        [shape(height, points), shape(nfreq, count, panel)],
        [kept, table, near1, far1],
        whole // 2,
    )
    near2, far2 = swap(own2, own2)

    def make_j(w_ref, near_ref, far_ref, s_ref, own_ref, tm_ref, out, g_out, u_out):
        kernel = from_above(near_ref, far_ref, 0, count)
        zero = jnp.zeros((count, points), BF)
        left = jnp.concatenate([kernel, zero], 0)
        right = jnp.concatenate([zero, kernel], 0)
        for f in range(nfreq):
            for c in range(2):
                row = f * panel + c * count
                out[row : row + count] = dot_t(kernel, w_ref[f, c]).astype(BF)
            g_out[f] = (
                dot_t(s_ref[f, 0:count], left) + dot_t(s_ref[f, count:panel], right)
            ).astype(BF)
            start1 = unpack(own_ref, body + f * rows, 0, count, width)
            u_out[f] = dot(tm_ref[f], both(start1)).astype(BF)

    j, g, tu1 = call(
        make_j,
        [
            shape(body, points),
            shape(nfreq, count, panel),
            shape(nfreq, count, width),
        ],
        [kept, near1, far1, seen, own2, tm],
        whole // 2,
    )

    def advance(w_ref, x, f):
        y = jnp.concatenate([-x[count:], x[:count]], 0)
        return (dot(x, w_ref[f, 0]) + dot(y, w_ref[f, 1])).astype(BF)

    def make_n(w_ref, t_ref, near_ref, far_ref, o_ref, j_ref, g_ref, out, x_out, y_out, u_out):
        even = is_even("depth")
        low = body + total

        def put(row, col, up, down):
            place = (slice(row, row + up.shape[0]), slice(col, col + up.shape[1]))
            x_out[place] = jnp.where(even, down, up)
            y_out[place] = jnp.where(even, up, down)

        angles = from_below(near_ref, far_ref, body, low)
        out[body:] = angles
        above = from_above(near_ref, far_ref, low, height)
        for f in range(nfreq):
            first_row = f * panel
            x = from_below(near_ref, far_ref, first_row, first_row + panel)
            n = advance(w_ref, x, f)
            out[first_row : first_row + panel] = n
            put(first_row, 0, n, j_ref[first_row : first_row + panel])
            pair = dot_t(t_ref[...], n).astype(BF)
            for i in range(count // 16):
                cut = slice(i * 16, (i + 1) * 16)
                put(low, f * spread + i * panel, g_ref[f, cut], pair[cut])
            start = unpack(o_ref, count + f * rows, 0, count, width)
            pair_above = unpack(above, 0, f * spread, count, panel)
            seen_above = dot(pair_above, both(start)).astype(BF)
            u_out[f] = seen_above
            for i in range(count // rows):
                cut = slice(i * rows, (i + 1) * rows)
                up = angles[f * rows : (f + 1) * rows, i * width : (i + 1) * width]
                put(body + f * rows, i * width, up, seen_above[cut])

    own3, x3, y3, tu1_above = call(
        make_n,
        [
            shape(body + total, points),
            shape(height, points),
            shape(height, points),
            shape(nfreq, count, width),
        ],
        [kept, table, near2, far2, own1, j, g],
        whole,
    )
    near3, far3 = swap(x3, y3)

    scale = float(1.0 / np.sqrt(np.float32(width // 2 * nfreq * lax.axis_size("freq"))))

    def make_q(
        w_ref, near_ref, far_ref, n_ref, m_ref, s_ref, g_ref, o_ref, u_ref, v_ref,
        q_out, f_out, c_out, a_out
    ):
        partial = jnp.zeros((count, points), F32)
        tail = from_below(near_ref, far_ref, body, height)
        above = from_above(near_ref, far_ref, body, height)
        for f in range(nfreq):
            j = from_above(near_ref, far_ref, f * panel, (f + 1) * panel)
            real = dot_t(s_ref[f, 0:count], j)
            imag = dot_t(s_ref[f, count:panel], j)
            h = (real + turned(imag)).astype(BF)
            tu1_two = unpack(above, f * rows, 0, count, width)
            low = body + f * rows
            start1 = unpack(m_ref, low, 0, count, width)
            pair = unpack(above, total, f * spread, count, panel)
            tu2_one = (dot(pair, both(start1)) + v_ref[f].astype(F32)).astype(BF)
            down3 = dot(h, both(tu1_two)) + dot(g_ref[f], both(tu2_one))
            start = unpack(o_ref, count + f * rows, 0, count, width)
            angles = (start.astype(F32) - down3).astype(BF)
            a_out[f] = angles

            n = from_below(near_ref, far_ref, f * panel, (f + 1) * panel)
            q = advance(w_ref, n, f)
            q_out[f] = q
            start2 = unpack(n_ref, low, 0, count, width)
            start3 = unpack(tail, f * rows, 0, count, width)
            turn = unpack(tail, total, f * spread, count, panel)
            down2 = dot(turn, both(u_ref[f]))
            shifted = (start1.astype(F32) - down2).astype(BF)
            fields = jnp.concatenate([both(start3), both(start2), both(shifted)], 0)
            f_out[f] = fields
            weight = dot_t(angles, fields).astype(BF)
            stack = jnp.concatenate(
                [q, n_ref[f * panel : (f + 1) * panel], m_ref[f * panel : (f + 1) * panel]], 0
            )
            partial = partial + dot(weight, stack)
        c_out[...] = (partial * scale).astype(BF)

    q, fields, partial, angles = call(
        make_q,
        [
            shape(nfreq, panel, points),
            shape(nfreq, 3 * panel, width),
            shape(count, points),
            shape(nfreq, count, width),
        ],
        [kept, near3, far3, own3, own2, seen, g, own1, tu1, tu1_above],
        whole + 5 * near,
    )

    def make_up(q_ref, n_ref, m_ref, f_ref, out):
        for f in range(nfreq):
            stack = jnp.concatenate(
                [
                    q_ref[f],
                    n_ref[f * panel : (f + 1) * panel],
                    m_ref[f * panel : (f + 1) * panel],
                ],
                0,
            )
            out[f] = t_dot(stack, f_ref[f]).astype(BF)

    (upgoing,) = call(
        make_up, [shape(nfreq, points, width)], [q, own3, own2, fields], 3 * near
    )

    size = lax.axis_size("freq")
    share = points // size
    def partner(value, step):
        return lax.ppermute(value, "freq", [(i, i ^ step) for i in range(size)])

    value, step = partial, size // 2
    while step > 2:
        value = (value.astype(F32) + partner(value, step).astype(F32)).astype(BF)
        step //= 2
    others = [partner(value, k) for k in range(1, 2 * step)]

    def last(c_ref, t_ref, a_ref, v_ref, *refs):
        *o_refs, out, g_out, keep = refs
        gradient = v_ref[...].astype(F32)
        for ref in o_refs:
            gradient = gradient + ref[...].astype(F32)
        keep[...] = gradient
        kernel = ((c_ref[...] - gradient) * t_ref[...].astype(F32)).astype(BF)
        for f in range(nfreq):
            out[f] = t_dot(kernel, a_ref[f]).astype(BF)
        begin = pl.multiple_of(lax.axis_index("freq") * share, share)
        g_out[...] = keep[:, pl.ds(begin, share)]

    reflected, mine = call(
        last,
        [shape(nfreq, points, width), shape(count, share, dtype=F32)],
        [coeffs, table, angles, value, *others],
        near,
        scratch=[pltpu.VMEM((count, points), F32)],
    )
    return (upgoing[None], mine.T[None], reflected[None])


def solution(mesh):
    return jax.shard_map(
        local,
        mesh=mesh,
        in_specs=(
            P("depth", "freq", None, None, None),
            P("depth", "freq", None, None),
            P("depth", None, None),
        ),
        out_specs=(
            P("depth", "freq", None, None),
            P("depth", "freq", None),
            P("depth", "freq", None, None),
        ),
        check_vma=False,
    )
```

```python
import jax
import jax.numpy as jnp
import numpy as np
from jax import lax
from jax.experimental import pallas as pl
from jax.experimental.pallas import tpu as pltpu
from jax.sharding import PartitionSpec as P

BF = jnp.bfloat16
F32 = jnp.float32
MIB = 2**20


def exchanged(block, axis, first):
    size = lax.axis_size(axis)
    route = []
    for i in range(first, size - 1, 2):
        route += [(i, i + 1), (i + 1, i)]
    return lax.ppermute(block, axis, route)


def is_even(axis):
    return lax.rem(lax.axis_index(axis), 2) == 0


def angle_table(count, points):
    angle = np.arange(count, dtype=np.float32)[:, None] + np.float32(0.5)
    place = np.arange(points, dtype=np.float32)[None, :] + np.float32(0.5)
    wave = np.cos(np.float32(np.pi) * angle * place / np.float32(points))
    return jnp.asarray((np.sqrt(np.float32(2.0 / points)) * wave).astype(BF))


def dot(a, b):
    return jnp.dot(a, b, preferred_element_type=F32)


def dot_t(a, b):
    return lax.dot_general(a, b, (((1,), (1,)), ((), ())), preferred_element_type=F32)


def t_dot(a, b):
    return lax.dot_general(a, b, (((0,), (0,)), ((), ())), preferred_element_type=F32)


def turned(field):
    half = field.shape[-1] // 2
    return jnp.concatenate([-field[:, half:], field[:, :half]], -1)


def both(field):
    return jnp.concatenate([field, turned(field)], 0)


def pack(ref, row, col, value):
    width = value.shape[1]
    fold = min((ref.shape[1] - col) // width, value.shape[0] // 16)
    rows = value.shape[0] // fold
    for i in range(fold):
        ref[row : row + rows, col + i * width : col + (i + 1) * width] = value[
            i * rows : (i + 1) * rows
        ]


def unpack(ref, row, col, count, width):
    fold = min((ref.shape[1] - col) // width, count // 16)
    rows = count // fold
    return jnp.concatenate(
        [
            ref[row : row + rows, col + i * width : col + (i + 1) * width]
            for i in range(fold)
        ],
        0,
    )


def folded_rows(count, width, points):
    return count // min(points // width, count // 16)


def call(body, outs, args, flops, vmem=12, scratch=(), hbm=()):
    spec = pl.BlockSpec(memory_space=pltpu.VMEM)
    anywhere = pl.BlockSpec(memory_space=pltpu.HBM)
    size = sum(int(np.prod(a.shape)) * a.dtype.itemsize for a in args)
    return pl.pallas_call(
        body,
        out_shape=outs,
        in_specs=[anywhere if i in hbm else spec for i in range(len(args))],
        out_specs=[spec] * len(outs),
        scratch_shapes=list(scratch),
        cost_estimate=pl.CostEstimate(flops=flops, bytes_accessed=size, transcendentals=0),
        compiler_params=pltpu.CompilerParams(vmem_limit_bytes=vmem * MIB),
    )(*args)


def shape(*dims, dtype=BF):
    return jax.ShapeDtypeStruct(dims, dtype)


def local(propagator, incident, coeffs):
    weights = propagator[0]
    source = incident[0]
    coeffs = coeffs[0].T
    count, points = coeffs.shape
    nfreq, _, width = source.shape
    table = angle_table(count, points)
    panel = 2 * count
    rows = folded_rows(count, width, points)
    total = nfreq * rows
    spread = panel * (count // 16)
    near = points * count * panel * nfreq * 2
    whole = nfreq * 2 * points * points * panel * 2

    def swap(x, y):
        far = exchanged(y, "depth", 1)
        near = exchanged(x, "depth", 0)
        return near, far

    def from_below(near_ref, far_ref, low, high):
        return jnp.where(is_even("depth"), near_ref[low:high], far_ref[low:high])

    def from_above(near_ref, far_ref, low, high):
        return jnp.where(is_even("depth"), far_ref[low:high], near_ref[low:high])

    hbm = pltpu.HBM

    def first(s_ref, c_ref, t_ref, out, table_out, src, coef, sems):
        copies = [
            pltpu.make_async_copy(t_ref, table_out, sems.at[0]),
            pltpu.make_async_copy(c_ref, coef, sems.at[1]),
            pltpu.make_async_copy(s_ref, src, sems.at[2]),
        ]
        for copy in copies:
            copy.start()
        copies[0].wait()
        copies[1].wait()
        out[0:count] = (coef[...] * table_out[...].astype(F32)).astype(BF)
        copies[2].wait()
        for f in range(nfreq):
            pack(out, count + f * rows, 0, dot(table_out[...], src[f]).astype(BF))

    own1, table = call(
        first,
        [shape(count + total, points), pltpu.VMEM((count, points), BF)],
        [pltpu.with_memory_space_constraint(x, hbm) for x in (source, coeffs, table)],
        near,
        scratch=[
            pltpu.VMEM(source.shape, BF),
            pltpu.VMEM(coeffs.shape, F32),
            pltpu.SemaphoreType.DMA((3,)),
        ],
        hbm=(0, 1, 2),
    )
    near1, far1 = swap(own1, own1)

    def load(w_ref, t_ref, kept, seen, sems):
        copies = [
            pltpu.make_async_copy(w_ref.at[f, c], kept.at[f, c], sems.at[2 * f + c])
            for f in range(nfreq)
            for c in range(2)
        ]
        for copy in copies:
            copy.start()
        for f in range(nfreq):
            for c in range(2):
                copies[2 * f + c].wait()
                seen[f, c * count : (c + 1) * count] = dot(t_ref[...], kept[f, c]).astype(BF)

    kept, seen = call(
        load,
        [pltpu.VMEM(weights.shape, BF), shape(nfreq, panel, points)],
        [pltpu.with_memory_space_constraint(weights, hbm), table],
        whole // 2,
        scratch=[pltpu.SemaphoreType.DMA((2 * nfreq,))],
        hbm=(0,),
    )
    body = nfreq * panel

    height = body + total + 16

    def make_m(w_ref, t_ref, near_ref, far_ref, out, tm):
        kernel = from_below(near_ref, far_ref, 0, count)
        out[body : body + total] = from_below(near_ref, far_ref, count, count + total)
        for f in range(nfreq):
            parts = [dot(kernel, w_ref[f, c]).astype(BF) for c in range(2)]
            m = jnp.concatenate(parts, 0)
            out[f * panel : (f + 1) * panel] = m
            pair = dot_t(t_ref[...], m).astype(BF)
            tm[f] = pair
            pack(out, body + total, f * spread, pair)

    own2, tm = call(
        make_m,
        [shape(height, points), shape(nfreq, count, panel)],
        [kept, table, near1, far1],
        whole // 2,
    )
    near2, far2 = swap(own2, own2)

    def make_j(w_ref, near_ref, far_ref, s_ref, own_ref, tm_ref, out, g_out, u_out):
        kernel = from_above(near_ref, far_ref, 0, count)
        zero = jnp.zeros((count, points), BF)
        left = jnp.concatenate([kernel, zero], 0)
        right = jnp.concatenate([zero, kernel], 0)
        for f in range(nfreq):
            for c in range(2):
                row = f * panel + c * count
                out[row : row + count] = dot_t(kernel, w_ref[f, c]).astype(BF)
            g_out[f] = (
                dot_t(s_ref[f, 0:count], left) + dot_t(s_ref[f, count:panel], right)
            ).astype(BF)
            start1 = unpack(own_ref, body + f * rows, 0, count, width)
            u_out[f] = dot(tm_ref[f], both(start1)).astype(BF)

    j, g, tu1 = call(
        make_j,
        [
            shape(body, points),
            shape(nfreq, count, panel),
            shape(nfreq, count, width),
        ],
        [kept, near1, far1, seen, own2, tm],
        whole // 2,
    )

    def advance(w_ref, x, f):
        y = jnp.concatenate([-x[count:], x[:count]], 0)
        return (dot(x, w_ref[f, 0]) + dot(y, w_ref[f, 1])).astype(BF)

    def make_n(w_ref, t_ref, near_ref, far_ref, o_ref, j_ref, g_ref, out, x_out, y_out, u_out):
        even = is_even("depth")
        low = body + total

        def put(row, col, up, down):
            place = (slice(row, row + up.shape[0]), slice(col, col + up.shape[1]))
            x_out[place] = jnp.where(even, down, up)
            y_out[place] = jnp.where(even, up, down)

        angles = from_below(near_ref, far_ref, body, low)
        out[body:] = angles
        above = from_above(near_ref, far_ref, low, height)
        for f in range(nfreq):
            first_row = f * panel
            x = from_below(near_ref, far_ref, first_row, first_row + panel)
            n = advance(w_ref, x, f)
            out[first_row : first_row + panel] = n
            put(first_row, 0, n, j_ref[first_row : first_row + panel])
            pair = dot_t(t_ref[...], n).astype(BF)
            for i in range(count // 16):
                cut = slice(i * 16, (i + 1) * 16)
                put(low, f * spread + i * panel, g_ref[f, cut], pair[cut])
            start = unpack(o_ref, count + f * rows, 0, count, width)
            pair_above = unpack(above, 0, f * spread, count, panel)
            seen_above = dot(pair_above, both(start)).astype(BF)
            u_out[f] = seen_above
            for i in range(count // rows):
                cut = slice(i * rows, (i + 1) * rows)
                up = angles[f * rows : (f + 1) * rows, i * width : (i + 1) * width]
                put(body + f * rows, i * width, up, seen_above[cut])

    own3, x3, y3, tu1_above = call(
        make_n,
        [
            shape(body + total, points),
            shape(height, points),
            shape(height, points),
            shape(nfreq, count, width),
        ],
        [kept, table, near2, far2, own1, j, g],
        whole,
    )
    near3, far3 = swap(x3, y3)

    def make_q_near(w_ref, near_ref, out):
        @pl.when(is_even("depth"))
        def _():
            for f in range(nfreq):
                out[f] = advance(w_ref, near_ref[f * panel : (f + 1) * panel], f)

        @pl.when(jnp.logical_not(is_even("depth")))
        def _():
            out[...] = jnp.zeros(out.shape, BF)

    (q_near,) = call(
        make_q_near, [shape(nfreq, panel, points)], [kept, near3], whole
    )

    scale = float(1.0 / np.sqrt(np.float32(width // 2 * nfreq * lax.axis_size("freq"))))

    def make_q(
        w_ref, near_ref, far_ref, n_ref, m_ref, s_ref, g_ref, o_ref, u_ref, v_ref, q_ref,
        q_out, f_out, c_out, a_out
    ):
        partial = jnp.zeros((count, points), F32)
        @pl.when(is_even("depth"))
        def _():
            q_out[...] = q_ref[...]

        @pl.when(jnp.logical_not(is_even("depth")))
        def _():
            for f in range(nfreq):
                q_out[f] = advance(w_ref, far_ref[f * panel : (f + 1) * panel], f)

        tail = from_below(near_ref, far_ref, body, height)
        above = from_above(near_ref, far_ref, body, height)
        for f in range(nfreq):
            j = from_above(near_ref, far_ref, f * panel, (f + 1) * panel)
            real = dot_t(s_ref[f, 0:count], j)
            imag = dot_t(s_ref[f, count:panel], j)
            h = (real + turned(imag)).astype(BF)
            tu1_two = unpack(above, f * rows, 0, count, width)
            low = body + f * rows
            start1 = unpack(m_ref, low, 0, count, width)
            pair = unpack(above, total, f * spread, count, panel)
            tu2_one = (dot(pair, both(start1)) + v_ref[f].astype(F32)).astype(BF)
            down3 = dot(h, both(tu1_two)) + dot(g_ref[f], both(tu2_one))
            start = unpack(o_ref, count + f * rows, 0, count, width)
            angles = (start.astype(F32) - down3).astype(BF)
            a_out[f] = angles

            q = q_out[f]
            start2 = unpack(n_ref, low, 0, count, width)
            start3 = unpack(tail, f * rows, 0, count, width)
            turn = unpack(tail, total, f * spread, count, panel)
            down2 = dot(turn, both(u_ref[f]))
            shifted = (start1.astype(F32) - down2).astype(BF)
            fields = jnp.concatenate([both(start3), both(start2), both(shifted)], 0)
            f_out[f] = fields
            weight = dot_t(angles, fields).astype(BF)
            stack = jnp.concatenate(
                [q, n_ref[f * panel : (f + 1) * panel], m_ref[f * panel : (f + 1) * panel]], 0
            )
            partial = partial + dot(weight, stack)
        c_out[...] = (partial * scale).astype(BF)

    q, fields, partial, angles = call(
        make_q,
        [
            shape(nfreq, panel, points),
            shape(nfreq, 3 * panel, width),
            shape(count, points),
            shape(nfreq, count, width),
        ],
        [kept, near3, far3, own3, own2, seen, g, own1, tu1, tu1_above, q_near],
        whole + 5 * near,
    )

    def make_up(q_ref, n_ref, m_ref, f_ref, out):
        for f in range(nfreq):
            stack = jnp.concatenate(
                [
                    q_ref[f],
                    n_ref[f * panel : (f + 1) * panel],
                    m_ref[f * panel : (f + 1) * panel],
                ],
                0,
            )
            out[f] = t_dot(stack, f_ref[f]).astype(BF)

    (upgoing,) = call(
        make_up, [shape(nfreq, points, width)], [q, own3, own2, fields], 3 * near
    )

    size = lax.axis_size("freq")
    share = points // size
    def partner(value, step):
        return lax.ppermute(value, "freq", [(i, i ^ step) for i in range(size)])

    value, step = partial, size // 2
    while step > 2:
        value = (value.astype(F32) + partner(value, step).astype(F32)).astype(BF)
        step //= 2
    others = [partner(value, k) for k in (1, 3, 2)[: 2 * step - 1]]

    def last(c_ref, t_ref, a_ref, v_ref, *refs):
        *o_refs, out, g_out, keep = refs
        gradient = v_ref[...].astype(F32)
        for ref in o_refs:
            gradient = gradient + ref[...].astype(F32)
        keep[...] = gradient
        kernel = ((c_ref[...] - gradient) * t_ref[...].astype(F32)).astype(BF)
        for f in range(nfreq):
            out[f] = t_dot(kernel, a_ref[f]).astype(BF)
        begin = pl.multiple_of(lax.axis_index("freq") * share, share)
        g_out[...] = keep[:, pl.ds(begin, share)]

    reflected, mine = call(
        last,
        [shape(nfreq, points, width), shape(count, share, dtype=F32)],
        [coeffs, table, angles, value, *others],
        near,
        scratch=[pltpu.VMEM((count, points), F32)],
    )
    return (upgoing[None], mine.T[None], reflected[None])


def solution(mesh):
    return jax.shard_map(
        local,
        mesh=mesh,
        in_specs=(
            P("depth", "freq", None, None, None),
            P("depth", "freq", None, None),
            P("depth", None, None),
        ),
        out_specs=(
            P("depth", "freq", None, None),
            P("depth", "freq", None),
            P("depth", "freq", None, None),
        ),
        check_vma=False,
    )
```
